32 devices in a mesh: groups: 2 (over x), dev: 16 (over z, y, core).
Axes of the slice: x: 2, y: 2, z: 4, core: 2. Of those that a mesh axis runs over, the one named last changes fastest.
Arguments:
- residual: bfloat16 [128, 3072], P('groups', 'dev'), parts along dimension 0, may hold values from -6 to 6
- queries: bfloat16 [32, 32, 768], P(('groups', 'dev')), parts along dimension 0, may hold values from -6 to 6
- kv_cache: bfloat16 [32, 2, 32, 128, 128], P(('groups', 'dev')), parts along dimension 0, may hold values from -6 to 6
- lengths: int32 [128], P('groups'), parts along dimension 0, may hold values from 2 to 128, as said below
- out_weight: bfloat16 [6144, 3072], P(None, 'dev'), may hold values from -0.078125 to 0.078125
- norm_gain: bfloat16 [3072], P('dev'), may hold values from 0.099609375 to 1.8984375
- router_weight: bfloat16 [3072, 8], P('dev'), may hold values from -0.109375 to 0.109375
- gate_weight: bfloat16 [3072, 65536], P(None, 'dev'), may hold values from -0.109375 to 0.109375
- up_weight: bfloat16 [3072, 65536], P(None, 'dev'), may hold values from -0.109375 to 0.109375
- down_weight: bfloat16 [65536, 3072], P('dev'), may hold values from -0.0625 to 0.0625
- expert_ids: int32 [128, 2], P('groups'), parts along dimension 0, may hold values from 0 to 7, all different within a row; in each aligned block of 64 rows (0 to 63, 64 to 127, ...) at most 32 rows name the same one
Outputs:
- layer_out: bfloat16 [128, 3072], P('groups', 'dev'), parts along dimension 0
The draws below stay inside these ranges and needn't reach their ends.
There are 2 independent parts, one for each index of `groups`. The reference program is written for one: setup_inputs(seed, part) draws one part's arguments, and reference() takes and returns one part's arrays. A program takes and returns all parts, laid end to end along the dimension named above; an argument that names none is the same for every part. Nothing has to cross between parts.
Inputs may be any that keep to these rules, and one draw needn't show every extreme that they name: Positions from lengths[r] on are unused; some row has all 128 positions valid. `expert_ids`: each row names two different experts; no expert is named by more than 32 rows, a bound that some block reaches.
All inputs are finite; a program needn't handle non-finite values.
Results may differ from the reference program's by a relative error of at most 0.0048.
Values may be sent and summed in bfloat16 or wider, within the bound.
A program may use at most 192 MiB of HBM per device.

```python
import functools
import math
import jax
import jax.numpy as jnp
import numpy as np
from jax import lax

D = 3072
QHEADS = 48
KVHEADS = 8
HEAD_DIM = 128
EXPERTS = 8
TOPK = 2
FF = 8192
ROWS_SH = 32
CACHE = 128
GROUP_Q = 6
ATT_SHARDS = 16
BATCH = 64
CAP = 32


def draw_queries(key, part):
    key = jax.random.fold_in(key, 11)
    shape = (ATT_SHARDS, ROWS_SH, GROUP_Q * HEAD_DIM)
    base = jnp.clip(jax.random.normal(key, shape, jnp.float32), -4.0, 4.0)
    return base.astype(jnp.bfloat16)


def draw_kv_cache(key, part):
    key = jax.random.fold_in(key, 23)
    shape = (ATT_SHARDS, 2, ROWS_SH, CACHE, HEAD_DIM)
    base = jnp.clip(jax.random.normal(key, shape, jnp.float32), -4.0, 4.0)
    return base.astype(jnp.bfloat16)


def draw_lengths(key, part):
    key = jax.random.fold_in(key, 5)
    drawn = jax.random.randint(key, (BATCH,), 2, CACHE + 1)
    return drawn.at[0].set(CACHE).astype(jnp.int32)


def block_scale(key, extent, split, low, largest):
    level = 1.0
    for axis_at, shards_of in split:
        steps = jax.random.uniform(jax.random.fold_in(jax.random.fold_in(key, 6), axis_at), (shards_of,), jnp.float32, low / len(split), largest / len(split))
        level = level * jnp.repeat(jnp.exp(steps), extent[axis_at] // shards_of).reshape((-1,) + (1,) * (len(extent) - 1 - axis_at))
    return level


def deal_out(stream_key, own, number, rows, amount, top, limit, lean):
    sequence = jax.random.permutation(stream_key, amount)
    packed, ordinary = shares(amount, rows * top, limit, lean, True), shares(amount, rows * top, limit, lean, False)
    places = jnp.arange(amount)

    def named(sizes, rotation):
        used = int((sizes > 0).sum())
        fixed = max(1, used // 4)
        shifted = fixed + (places - fixed + rotation * (used - fixed)) % max(1, amount - fixed)
        return jnp.zeros((amount,), jnp.int32).at[sequence[jnp.where(places < fixed, places, shifted)]].set(jnp.asarray(sizes, jnp.int32))

    sizes = jnp.where(number % 4 == 0, named(packed, number // 4), named(ordinary, number - number // 4 - 1))
    mixed = jax.random.permutation(jax.random.fold_in(own, 3), amount)
    source_of, receiver = mixed[0:amount // 2 * 2:2], mixed[1:amount // 2 * 2:2]
    room = jnp.minimum(sizes[source_of] - 1, limit - sizes[receiver]) // 2
    room = jnp.where((source_of == sequence[0]) | (receiver == sequence[0]) | (sizes[receiver] == 0), 0, jnp.maximum(room, 0))
    shifted = jax.random.randint(jax.random.fold_in(own, 4), (amount // 2,), 0, 1 << 20) % (room + 1)
    sizes = sizes.at[source_of].add(-shifted).at[receiver].add(shifted)
    members = jnp.searchsorted(jnp.cumsum(sizes), jnp.arange(rows * top), side="right").astype(jnp.int32)
    listing = members.reshape(top, rows).T
    listing = listing[jax.random.permutation(jax.random.fold_in(own, 1), rows)]
    rotation = jax.random.randint(jax.random.fold_in(own, 2), (rows, 1), 0, top)
    return jnp.take_along_axis(listing, (jnp.arange(top)[None, :] + rotation) % top, axis=1)


def shares(count, total, reach, lean, full):
    weights = [(1 << 20) // math.isqrt(standing ** lean) + 1 for standing in range(1, count + 1)]
    largest = reach if full else min(reach, max(-(-total // count), total * weights[0] // sum(weights)))
    least = 1 if total - largest >= count - 1 else 0
    given, rest = [largest] + [least] * (count - 1), total - largest - least * (count - 1)
    while rest > 0:
        movable = [i for i in range(1, count) if given[i] < largest] or [i for i in range(1, count) if given[i] < reach]
        mass, remaining = sum([weights[i] for i in movable]), rest
        for i in movable:
            addition = min(reach - given[i], max(1, remaining * weights[i] // mass), rest)
            given[i] = given[i] + addition
            rest = rest - addition
    return np.array(given)


def bell_draw(rng, extent, scale, bound, split=(), held_as=jnp.bfloat16):
    values = scale * jax.random.normal(rng, extent, jnp.float32)
    if split:
        values = values * block_scale(rng, extent, split, -0.22, 0.18)
    return jnp.clip(values, -bound, bound).astype(held_as)


def setup_inputs(seed: int = 0, part: int = 0) -> dict:
    seeds = jax.random.split(jax.random.key(seed), 12)
    part_splits = jax.random.split(jax.random.fold_in(seeds[11], part), 12)
    residual = bell_draw(part_splits[0], (BATCH, D), 1.0, 6.0, ((1, 16),))
    queries = draw_queries(jax.random.fold_in(jax.random.fold_in(seeds[11], part), 71), part)
    kv_cache = draw_kv_cache(jax.random.fold_in(jax.random.fold_in(seeds[11], part), 71), part)
    lengths = draw_lengths(jax.random.fold_in(jax.random.fold_in(seeds[11], part), 71), part)
    out_weight = bell_draw(seeds[4], (QHEADS * HEAD_DIM, D), (QHEADS * HEAD_DIM) ** -0.5, 0.078125, ((1, 16),))
    norm_gain = jnp.clip(1.0 + 0.18 * jax.random.normal(seeds[5], (D,), jnp.float32), 0.099609375, 1.8984375).astype(jnp.bfloat16)
    router_weight = bell_draw(seeds[6], (D, EXPERTS), D ** -0.5, 0.109375, ((0, 16),))
    gate_weight = bell_draw(seeds[7], (D, EXPERTS * FF), D ** -0.5, 0.109375, ((1, 16),))
    up_weight = bell_draw(seeds[8], (D, EXPERTS * FF), D ** -0.5, 0.109375, ((1, 16),))
    down_weight = bell_draw(seeds[9], (EXPERTS * FF, D), FF ** -0.5, 0.0625, ((0, 16),))
    expert_ids_keys = jax.random.split(jax.random.fold_in(part_splits[10], 1), BATCH // BATCH)
    expert_ids_turns = jax.random.permutation(jax.random.fold_in(part_splits[10], 3), BATCH // BATCH)
    expert_ids = jax.vmap(lambda own, number: deal_out(jax.random.fold_in(part_splits[10], 2), own, number, BATCH, EXPERTS, TOPK, CAP, 1))(expert_ids_keys, expert_ids_turns).reshape((BATCH, TOPK))
    return {"residual": residual, "queries": queries, "kv_cache": kv_cache, "lengths": lengths, "out_weight": out_weight, "norm_gain": norm_gain, "router_weight": router_weight, "gate_weight": gate_weight, "up_weight": up_weight, "down_weight": down_weight, "expert_ids": expert_ids}


def attend_block(block, queries, kv_cache, lengths):
    first_row = (block // KVHEADS * ROWS_SH).astype(jnp.int32)
    row_lengths = lax.dynamic_slice_in_dim(lengths, first_row, ROWS_SH)
    query_block = queries[block].astype(jnp.float32).reshape(ROWS_SH, GROUP_Q, HEAD_DIM)
    key_block = kv_cache[block, 0].astype(jnp.float32)
    value_block = kv_cache[block, 1].astype(jnp.float32)
    scores = jnp.einsum('thd,tld->thl', query_block, key_block) / math.sqrt(HEAD_DIM)
    valid = jnp.arange(CACHE)[None, None, :] < row_lengths[:, None, None]
    scores = jnp.where(valid, scores, -1e+30)
    row_top = lax.optimization_barrier(jnp.max(scores, axis=2, keepdims=True))
    expo = jnp.where(valid, jnp.exp(scores - row_top), 0.0)
    probs = (expo / lax.optimization_barrier(jnp.sum(expo, axis=2, keepdims=True))).astype(jnp.bfloat16)
    mixed_heads = jnp.einsum('thl,tld->thd', probs.astype(jnp.float32), value_block)
    return mixed_heads.reshape(ROWS_SH, GROUP_Q * HEAD_DIM).astype(jnp.bfloat16)

def slot_tables(expert_ids, logits, slot_count):
    numbers = jnp.arange(EXPERTS)
    pick_first = (expert_ids[:, 0:1] == numbers[None, :]).astype(jnp.float32)
    pick_second = (expert_ids[:, 1:2] == numbers[None, :]).astype(jnp.float32)
    logit_first = lax.optimization_barrier(jnp.sum(logits * pick_first, axis=1))
    logit_second = lax.optimization_barrier(jnp.sum(logits * pick_second, axis=1))
    gate_first = 1.0 / (1.0 + jnp.exp(logit_second - logit_first))
    gate_second = 1.0 / (1.0 + jnp.exp(logit_first - logit_second))
    routed = pick_first + pick_second
    gate_table = pick_first * gate_first[:, None] + pick_second * gate_second[:, None]
    ranks = jnp.cumsum(routed, axis=0) - routed
    slot_numbers = jnp.arange(slot_count).astype(jnp.float32)
    slot_table = routed.T[:, None, :] * (ranks.T[:, None, :] == slot_numbers[None, :, None]).astype(jnp.float32)
    slot_gate = jnp.einsum('esb,be->es', slot_table, gate_table, precision=lax.Precision.HIGHEST)
    return (slot_table, slot_gate)

def reference(residual, queries, kv_cache, lengths, out_weight, norm_gain, router_weight, gate_weight, up_weight, down_weight, expert_ids):
    attend = functools.partial(attend_block, queries=queries, kv_cache=kv_cache, lengths=lengths)
    blocks = lax.map(attend, jnp.arange(ATT_SHARDS, dtype=jnp.int32))
    shard_count = ATT_SHARDS // KVHEADS
    heads_out = blocks.reshape(shard_count, KVHEADS, ROWS_SH, GROUP_Q * HEAD_DIM).transpose(0, 2, 1, 3).reshape(BATCH, QHEADS * HEAD_DIM)
    attended = jnp.dot(heads_out, out_weight, preferred_element_type=jnp.float32)
    hidden_state = residual.astype(jnp.float32) + attended
    scale = lax.rsqrt(lax.optimization_barrier(jnp.mean(hidden_state * hidden_state, axis=1)) + 1e-05)
    normed = hidden_state * scale[:, None] * norm_gain.astype(jnp.float32)[None, :]
    logits = jnp.dot(normed, router_weight.astype(jnp.float32), precision=lax.Precision.HIGHEST)
    expert_in = normed.astype(jnp.bfloat16)
    slot_table, slot_gate = slot_tables(expert_ids, logits, CAP)

    def run_expert(expert):
        chooser = lax.dynamic_index_in_dim(slot_table, expert, 0, keepdims=False).astype(jnp.bfloat16)
        slot_in = jnp.dot(chooser, expert_in, preferred_element_type=jnp.float32).astype(jnp.bfloat16)
        start = (expert * FF).astype(jnp.int32)
        gate_cols = lax.dynamic_slice_in_dim(gate_weight, start, FF, 1)
        up_cols = lax.dynamic_slice_in_dim(up_weight, start, FF, 1)
        down_rows = lax.dynamic_slice_in_dim(down_weight, start, FF, 0)
        gate_part = jnp.dot(slot_in, gate_cols, preferred_element_type=jnp.float32)
        up_part = jnp.dot(slot_in, up_cols, preferred_element_type=jnp.float32)
        activation = (jax.nn.silu(gate_part) * up_part).astype(jnp.bfloat16)
        expert_out = jnp.dot(activation, down_rows, preferred_element_type=jnp.float32)
        weights_here = lax.dynamic_index_in_dim(slot_gate, expert, 0, keepdims=False)
        return expert_out * weights_here[:, None]
    outputs = lax.map(run_expert, jnp.arange(EXPERTS, dtype=jnp.int32))
    moe = jnp.einsum('esb,esd->bd', slot_table, outputs, precision=lax.Precision.HIGHEST)
    return (hidden_state + moe).astype(jnp.bfloat16)
```

```python
import math

import jax
import jax.numpy as jnp
from jax import lax
from jax.experimental import pallas as pl
from jax.experimental.pallas import tpu as pltpu
from jax.sharding import PartitionSpec as P

D = 3072
KVHEADS = 8
HEAD_DIM = 128
EXPERTS = 8
GROUP_Q = 6


def attend(query_block, cache_block, row_lengths):
    shard_rows = query_block.shape[0]
    query_heads = query_block.reshape(shard_rows, GROUP_Q, HEAD_DIM)
    key_block = cache_block[0]
    value_block = cache_block[1]
    scores = jnp.einsum(
        "thd,tld->thl", query_heads, key_block, preferred_element_type=jnp.float32
    ) / math.sqrt(HEAD_DIM)
    positions = jnp.arange(key_block.shape[1])
    valid = positions[None, None, :] < row_lengths[:, None, None]
    scores = jnp.where(valid, scores, -1e30)
    row_top = jnp.max(scores, axis=2, keepdims=True)
    expo = jnp.where(valid, jnp.exp(scores - row_top), 0.0)
    probs = (expo / jnp.sum(expo, axis=2, keepdims=True)).astype(jnp.bfloat16)
    mixed_heads = jnp.einsum("thl,tld->thd", probs, value_block, preferred_element_type=jnp.float32)
    return mixed_heads.reshape(shard_rows, GROUP_Q * HEAD_DIM).astype(jnp.bfloat16)


def slot_tables(expert_ids, logits, slot_count):
    numbers = jnp.arange(EXPERTS)
    pick_first = (expert_ids[:, 0:1] == numbers[None, :]).astype(jnp.float32)
    pick_second = (expert_ids[:, 1:2] == numbers[None, :]).astype(jnp.float32)
    logit_first = jnp.sum(logits * pick_first, axis=1)
    logit_second = jnp.sum(logits * pick_second, axis=1)
    gate_first = 1.0 / (1.0 + jnp.exp(logit_second - logit_first))
    gate_second = 1.0 / (1.0 + jnp.exp(logit_first - logit_second))
    routed = pick_first + pick_second
    gate_table = pick_first * gate_first[:, None] + pick_second * gate_second[:, None]
    ranks = jnp.cumsum(routed, axis=0) - routed
    slot_numbers = jnp.arange(slot_count).astype(jnp.float32)
    slot_table = routed.T[:, None, :] * (ranks.T[:, None, :] == slot_numbers[None, :, None]).astype(
        jnp.float32
    )
    slot_gate = jnp.einsum("esb,be->es", slot_table, gate_table, precision=lax.Precision.HIGHEST)
    return (slot_table, slot_gate)


def integer_ranks(expert_ids):
    numbers = jnp.arange(EXPERTS, dtype=jnp.int32)
    routed_int = (expert_ids[:, 0:1] == numbers[None, :]).astype(jnp.int32) + (
        expert_ids[:, 1:2] == numbers[None, :]
    ).astype(jnp.int32)
    ranks_int = jnp.cumsum(routed_int, axis=0) - routed_int
    return (routed_int, ranks_int)


def run_expert(slot_in, gate_weight, up_weight, down_weight, weights_here):
    gate_part = jnp.dot(slot_in, gate_weight, preferred_element_type=jnp.float32)
    up_part = jnp.dot(slot_in, up_weight, preferred_element_type=jnp.float32)
    activation = (jax.nn.silu(gate_part) * up_part).astype(jnp.bfloat16)
    expert_out = jnp.dot(activation, down_weight, preferred_element_type=jnp.float32)
    return expert_out * weights_here[:, None]


def on_device(
    residual,
    queries,
    kv_cache,
    lengths,
    out_weight,
    norm_gain,
    router_weight,
    gate_weight,
    up_weight,
    down_weight,
    expert_ids,
):
    devices = lax.axis_size("dev")
    my_index = lax.axis_index("dev")
    shard_rows = queries.shape[1]
    group_width = queries.shape[2]
    batch_rows = residual.shape[0]
    column_count = residual.shape[1]
    slot_count = batch_rows // 2
    per_expert = devices // EXPERTS
    my_expert = my_index // per_expert
    row_lengths = lax.dynamic_slice_in_dim(lengths, my_index // KVHEADS * shard_rows, shard_rows)
    heads_local = attend(queries[0], kv_cache[0], row_lengths)
    gathered = lax.all_gather(heads_local, "dev", axis=0, tiled=True)
    gathered = gathered.reshape(devices // KVHEADS, KVHEADS, shard_rows, group_width)
    weight_blocks = out_weight.reshape(KVHEADS, group_width, column_count)
    attended = jnp.einsum(
        "bgtk,gkc->btc", gathered, weight_blocks, preferred_element_type=jnp.float32
    )
    attended = attended.reshape(batch_rows, column_count)
    hidden_state = residual.astype(jnp.float32) + attended
    gain_cols = norm_gain.astype(jnp.float32)[None, :]
    router_cols = router_weight.astype(jnp.float32)
    squares_local = jnp.sum(hidden_state * hidden_state, axis=1)
    square_total = lax.psum(squares_local, "dev")
    scale = lax.rsqrt(square_total / D + 1e-05)
    normed = hidden_state * scale[:, None] * gain_cols
    logits = lax.psum(jnp.dot(normed, router_cols, precision=lax.Precision.HIGHEST), "dev")
    expert_in = normed.astype(jnp.bfloat16)
    slot_table, slot_gate = slot_tables(expert_ids, logits, slot_count)
    routed_int, ranks_int = integer_ranks(expert_ids)
    weights_here = lax.dynamic_index_in_dim(slot_gate, my_expert, 0, keepdims=False)
    picked = jnp.einsum(
        "esb,bc->sec",
        slot_table.astype(jnp.bfloat16),
        expert_in,
        preferred_element_type=jnp.float32,
    ).astype(jnp.bfloat16)
    outgoing = jnp.broadcast_to(
        picked[:, :, None, :], (slot_count, EXPERTS, per_expert, column_count)
    )
    outgoing = outgoing.reshape(slot_count, devices * column_count)
    slot_in = lax.all_to_all(outgoing, "dev", split_axis=1, concat_axis=1, tiled=True)
    expert_out = run_expert(slot_in, gate_weight, up_weight, down_weight, weights_here)
    returned = lax.all_to_all(expert_out, "dev", split_axis=1, concat_axis=1, tiled=True)
    summed = jnp.sum(returned.reshape(slot_count, EXPERTS, per_expert, column_count), axis=2)
    first_expert = expert_ids[:, 0]
    second_expert = expert_ids[:, 1]
    first_rank = jnp.take_along_axis(ranks_int, first_expert[:, None], axis=1)[:, 0]
    second_rank = jnp.take_along_axis(ranks_int, second_expert[:, None], axis=1)[:, 0]
    moe = summed[first_rank, first_expert] + summed[second_rank, second_expert]
    return (hidden_state + moe).astype(jnp.bfloat16)


ZS = 4
YS = 2
CHIPS = ZS * YS
DEVS = 2 * CHIPS
ROWS = 64
SLOTS = 32
BLOCK_ROWS = 32
COLS = 192
PAIR = 2 * COLS
HALF_W = 256
HEADS_W = GROUP_Q * HEAD_DIM
FF_LOCAL = 4096
FF_STEP = 512
FF_STEPS = FF_LOCAL // FF_STEP
UP_SLOTS = 6
DOWN_SLOTS = 5
F32 = jnp.float32
BF16 = jnp.bfloat16
NT = (((1,), (1,)), ((), ()))


def iota(shape, dim):
    return lax.broadcasted_iota(jnp.int32, shape, dim)


def fused_kernel(
    lengths,
    ids,
    residual,
    gain,
    router,
    q_hbm,
    kv_hbm,
    ow_hbm,
    gate_hbm,
    up_hbm,
    down_hbm,
    out,
    q_in,
    kv,
    ow,
    gu,
    dn,
    qs,
    lens,
    heads,
    gt,
    wide,
    picks,
    xb,
    stat_out,
    stats,
    xfull,
    act,
    rs,
    ret,
    in_sem,
    gu_sem,
    dn_sem,
    h_send,
    h_recv,
    x_send,
    x_recv,
    s_send,
    s_recv,
    r_send,
    r_recv,
):
    me = lax.axis_index("dev")
    core = lax.rem(me, 2)
    chip = me // 2
    y = lax.rem(chip, YS)
    z = chip // YS
    sibling = chip * 2 + (1 - core)

    def dev_of(zz, yy, cc):
        return (zz * YS + yy) * 2 + cc

    def remote(source, target, send, recv, device):
        return pltpu.make_async_remote_copy(
            src_ref=source,
            dst_ref=target,
            send_sem=send,
            recv_sem=recv,
            device_id={"dev": device},
            device_id_type=pl.DeviceIdType.MESH,
        )

    q_copy = pltpu.make_async_copy(q_hbm.at[0], q_in, in_sem.at[0])
    kv_copy = pltpu.make_async_copy(kv_hbm.at[0], kv, in_sem.at[1])
    ow_copy = pltpu.make_async_copy(ow_hbm, ow, in_sem.at[2])
    q_copy.start()
    kv_copy.start()

    barrier = pltpu.get_barrier_semaphore()
    for k in range(1, DEVS):
        pl.semaphore_signal(
            barrier,
            inc=1,
            device_id={"dev": lax.rem(me + k, DEVS)},
            device_id_type=pl.DeviceIdType.MESH,
        )

    def gu_copy(j, which):
        slot = lax.rem(j, UP_SLOTS)
        start = pl.multiple_of(j * FF_STEP, FF_STEP)
        origin = up_hbm if which else gate_hbm
        return pltpu.make_async_copy(
            origin.at[:, pl.ds(start, FF_STEP)], gu.at[slot, which], gu_sem.at[slot, which]
        )

    def down_chip(d):
        return lax.rem(chip + d + 1, CHIPS)

    def dn_copy(d):
        slot = lax.rem(d, DOWN_SLOTS)
        start = pl.multiple_of(down_chip(d) * PAIR, 128)
        return pltpu.make_async_copy(
            down_hbm.at[:, pl.ds(start, PAIR)], dn.at[slot], dn_sem.at[slot]
        )

    my_rows = (me // KVHEADS) * BLOCK_ROWS
    for t in range(BLOCK_ROWS):
        lens[t] = jnp.full((8, 128), lengths[my_rows + t], jnp.int32)

    lane = iota((ROWS, 128), 1)
    routed = jnp.where((ids[:, 0:1] == lane) | (ids[:, 1:2] == lane), 1.0, 0.0)
    tri = jnp.where(iota((ROWS, ROWS), 0) > iota((ROWS, ROWS), 1), 1.0, 0.0).astype(BF16)
    rank = jnp.dot(tri, routed.astype(BF16), preferred_element_type=F32)
    code = (routed * (rank + 1.0)).astype(BF16)
    owner = iota((128, EXPERTS * SLOTS), 0) * SLOTS
    place = iota((128, EXPERTS * SLOTS), 1)
    spread = jnp.where((place >= owner) & (place < owner + SLOTS), 1.0, 0.0).astype(BF16)
    spread_code = jnp.dot(code, spread, preferred_element_type=F32)
    slot_number = (jnp.bitwise_and(iota((ROWS, EXPERTS * SLOTS), 1), SLOTS - 1) + 1).astype(F32)
    table = jnp.where(spread_code == slot_number, 1.0, 0.0)
    table_pad = jnp.concatenate([table, jnp.zeros_like(table)], axis=0)
    gt[...] = jnp.transpose(table_pad)
    routed_pad = jnp.concatenate([routed, jnp.zeros_like(routed)], axis=0).astype(BF16)

    q_copy.wait()
    qs[...] = jnp.zeros_like(qs)
    for j in range(GROUP_Q):
        qs[:, j, :] = q_in[:, j * HEAD_DIM : (j + 1) * HEAD_DIM].astype(F32)
    kv_copy.wait()
    ow_copy.start()
    for j in range(UP_SLOTS):
        gu_copy(j, 0).start()
        gu_copy(j, 1).start()
    for d in range(DOWN_SLOTS):
        dn_copy(d).start()

    scores = jnp.einsum(
        "thd,tld->thl", qs[...].astype(BF16), kv[0], preferred_element_type=F32
    ) * (1.0 / math.sqrt(HEAD_DIM))
    valid = iota((BLOCK_ROWS, 8, 128), 2) < lens[...]
    scores = jnp.where(valid, scores, -1e30)
    top = jnp.max(scores, axis=2, keepdims=True)
    expo = jnp.where(valid, jnp.exp(scores - top), 0.0)
    probs = (expo / jnp.sum(expo, axis=2, keepdims=True)).astype(BF16)
    qs[...] = jnp.einsum("thl,tld->thd", probs, kv[1], preferred_element_type=F32)
    for j in range(GROUP_Q):
        heads[me, :, j * HEAD_DIM : (j + 1) * HEAD_DIM] = qs[:, j, :].astype(BF16)

    pl.semaphore_wait(barrier, DEVS - 1)

    def head_copy(block, number, device):
        return remote(
            heads.at[block], heads.at[block], h_send.at[number], h_recv.at[block], device
        )

    sent = []

    def send_heads(block, device):
        copy = head_copy(block, len(sent), device)
        copy.start()
        sent.append(copy)

    for k in (2, 1, 3):
        send_heads(me, dev_of(lax.rem(z + k, ZS), y, core))
    send_heads(me, dev_of(z, 1 - y, core))
    send_heads(me, sibling)
    for k in (1, 3, 2):
        block = dev_of(lax.rem(z + k, ZS), y, core)
        head_copy(block, 0, sibling).wait_recv()
        send_heads(block, dev_of(z, 1 - y, core))
        send_heads(block, sibling)
    for k in (0, 1, 3, 2):
        block = dev_of(lax.rem(z + k, ZS), 1 - y, core)
        head_copy(block, 0, sibling).wait_recv()
        send_heads(block, sibling)
    for k in (0, 1, 3, 2):
        for yy in (y, 1 - y):
            block = dev_of(lax.rem(z + k, ZS), yy, 1 - core)
            head_copy(block, 0, sibling).wait_recv()

    ow_copy.wait()
    attended = jnp.zeros((ROWS, COLS), F32)
    for g in range(KVHEADS):
        both = jnp.concatenate([heads[g], heads[KVHEADS + g]], axis=0)
        attended += jnp.dot(
            both, ow[g * HEADS_W : (g + 1) * HEADS_W, :], preferred_element_type=F32
        )
    hidden = residual[...].astype(F32) + attended
    gained = hidden * gain[...].astype(F32)

    wide[...] = jnp.zeros_like(wide)
    wide[0:ROWS, 0:COLS] = gained
    shifted = pltpu.roll(wide[...], core * 64, 1)
    picked = jnp.dot(gt[...].astype(BF16), shifted.astype(BF16), preferred_element_type=F32)
    picks[...] = picked.astype(BF16).reshape(EXPERTS, SLOTS, HALF_W)

    router_cols = jnp.transpose(
        jnp.concatenate([router[...].astype(F32), jnp.zeros((COLS, 120), F32)], axis=1)
    )[0:8]
    none = jnp.zeros_like(hidden)
    stat_out[...] = lax.dot_general(
        router_cols,
        jnp.concatenate([gained, none], axis=0),
        NT,
        precision=lax.Precision.HIGHEST,
        preferred_element_type=F32,
    ) + lax.dot_general(
        jnp.ones((8, COLS), F32),
        jnp.concatenate([none, hidden * hidden], axis=0),
        NT,
        precision=lax.Precision.HIGHEST,
        preferred_element_type=F32,
    )

    sent_x = []

    def row_copies(cc, source_chip, source, stat_source, number, device):
        at = cc * CHIPS + source_chip
        return (
            remote(source, xb.at[cc, source_chip], x_send.at[number], x_recv.at[at], device),
            remote(stat_source, stats.at[cc, source_chip], s_send.at[number], s_recv.at[at], device),
        )

    def send_rows(cc, source_chip, source, stat_source, device):
        copies = row_copies(cc, source_chip, source, stat_source, len(sent_x), device)
        for copy in copies:
            copy.start()
        sent_x.append(copies)

    def wait_rows(cc, source_chip):
        for copy in row_copies(
            cc, source_chip, xb.at[cc, source_chip], stats.at[cc, source_chip], 0, sibling
        ):
            copy.wait_recv()

    for k in (4, 3, 5, 2, 6, 1, 7):
        to = lax.rem(chip + k, CHIPS)
        send_rows(core, chip, picks.at[to], stat_out, to * 2 + core)
    send_rows(core, chip, picks.at[chip], stat_out, sibling)
    xb[core, chip] = picks[chip]
    stats[core, chip] = stat_out[...]
    for k in (1, 7, 2, 6, 3, 5, 4):
        source_chip = lax.rem(chip + k, CHIPS)
        wait_rows(core, source_chip)
        send_rows(
            core,
            source_chip,
            xb.at[core, source_chip],
            stats.at[core, source_chip],
            sibling,
        )
    for k in (0, 1, 7, 2, 6, 3, 5, 4):
        wait_rows(1 - core, lax.rem(chip + k, CHIPS))

    for s in range(CHIPS):
        at = s * PAIR
        xfull[:, at : at + 128] = xb[0, s, :, 0:128]
        xfull[:, at + 128 : at + 256] = xb[0, s, :, 128:256] + xb[1, s, :, 0:128]
        xfull[:, at + 256 : at + 384] = xb[1, s, :, 128:256]
    total = jnp.sum(stats[...].reshape(DEVS, 8, 128), axis=0)
    total = jnp.concatenate([total, jnp.zeros((120, 128), F32)], axis=0)
    mine = gt[pl.ds(pl.multiple_of(chip * SLOTS, SLOTS), SLOTS), :]
    slot_logits = lax.dot_general(
        mine, total, NT, precision=lax.Precision.HIGHEST, preferred_element_type=F32
    )
    slot_squares = lax.dot_general(
        pltpu.roll(mine, 64, 1),
        total,
        NT,
        precision=lax.Precision.HIGHEST,
        preferred_element_type=F32,
    )
    scale = lax.rsqrt(slot_squares[:, 0:1] / D + 1e-05)
    slot_experts = jnp.dot(mine.astype(BF16), routed_pad, preferred_element_type=F32)
    number = iota((SLOTS, 128), 1)
    own_logit = jnp.sum(jnp.where(number == chip, slot_logits, 0.0), axis=1, keepdims=True)
    other_logit = jnp.sum(
        jnp.where(number == chip, 0.0, slot_logits * slot_experts), axis=1, keepdims=True
    )
    weight = 1.0 / (1.0 + jnp.exp((other_logit - own_logit) * scale))

    def up_step(j):
        slot = lax.rem(j, UP_SLOTS)
        gu_copy(j, 0).wait()
        gu_copy(j, 1).wait()
        rows_in = xfull[...]
        gate_part = jnp.dot(rows_in, gu[slot, 0], preferred_element_type=F32) * scale
        up_part = jnp.dot(rows_in, gu[slot, 1], preferred_element_type=F32) * scale
        silu = gate_part / (1.0 + jnp.exp(-gate_part))
        act[:, pl.ds(pl.multiple_of(j * FF_STEP, FF_STEP), FF_STEP)] = (silu * up_part).astype(BF16)

    @pl.loop(0, FF_STEPS - UP_SLOTS)
    def _(j):
        up_step(j)
        gu_copy(j + UP_SLOTS, 0).start()
        gu_copy(j + UP_SLOTS, 1).start()

    @pl.loop(FF_STEPS - UP_SLOTS, FF_STEPS)
    def _(j):
        up_step(j)

    def return_copy(d, cc):
        return remote(
            rs.at[d, :, cc * 128 : cc * 128 + HALF_W],
            ret.at[core, chip],
            r_send.at[d, cc],
            r_recv.at[core * CHIPS + chip],
            down_chip(d) * 2 + cc,
        )

    def down_step(d):
        dn_copy(d).wait()
        part = jnp.dot(act[...], dn[lax.rem(d, DOWN_SLOTS)], preferred_element_type=F32)
        rs[d] = (part * weight).astype(BF16)

    @pl.loop(0, CHIPS - DOWN_SLOTS)
    def _(d):
        down_step(d)
        return_copy(d, 0).start()
        return_copy(d, 1).start()
        dn_copy(d + DOWN_SLOTS).start()

    @pl.loop(CHIPS - DOWN_SLOTS, CHIPS - 1)
    def _(d):
        down_step(d)
        return_copy(d, 0).start()
        return_copy(d, 1).start()

    last = CHIPS - 1
    down_step(last)

    def to_sibling(lanes):
        return remote(
            rs.at[last, :, lanes],
            ret.at[core, chip],
            r_send.at[last, 0],
            r_recv.at[core * CHIPS + chip],
            sibling,
        )

    @pl.when(core == 0)
    def _():
        to_sibling(slice(128, 384)).start()
        ret[core, chip] = rs[last, :, 0:256]

    @pl.when(core == 1)
    def _():
        to_sibling(slice(0, 256)).start()
        ret[core, chip] = rs[last, :, 128:384]

    def wait_return(cc, source_chip):
        remote(
            rs.at[0, :, 0:HALF_W],
            ret.at[cc, source_chip],
            r_send.at[0, 0],
            r_recv.at[cc * CHIPS + source_chip],
            sibling,
        ).wait_recv()

    for k in range(1, CHIPS):
        for cc in range(2):
            wait_return(cc, lax.rem(chip + k, CHIPS))
    wait_return(1 - core, chip)

    table_bf = table.astype(BF16)
    moe = jnp.zeros((ROWS, HALF_W), F32)
    for cc in range(2):
        moe += jnp.dot(
            table_bf, ret[cc].reshape(EXPERTS * SLOTS, HALF_W), preferred_element_type=F32
        )
    moe = pltpu.roll(moe, core * (HALF_W - 64), 1)
    out[...] = (hidden + moe[:, 0:COLS]).astype(BF16)

    for copy in sent:
        copy.wait_send()
    for copies in sent_x:
        for copy in copies:
            copy.wait_send()

    @pl.loop(0, last)
    def _(d):
        return_copy(d, 0).wait_send()
        return_copy(d, 1).wait_send()

    to_sibling(slice(0, 256)).wait_send()


def fused(
    residual,
    queries,
    kv_cache,
    lengths,
    out_weight,
    norm_gain,
    router_weight,
    gate_weight,
    up_weight,
    down_weight,
    expert_ids,
):
    vmem = pl.BlockSpec(memory_space=pltpu.VMEM)
    anywhere = pl.BlockSpec(memory_space=pl.ANY)
    dma = pltpu.SemaphoreType.DMA
    return pl.pallas_call(
        fused_kernel,
        out_shape=jax.ShapeDtypeStruct((ROWS, COLS), BF16),
        in_specs=[pl.BlockSpec(memory_space=pltpu.SMEM)] + [vmem] * 4 + [anywhere] * 6,
        out_specs=vmem,
        scratch_shapes=[
            pltpu.VMEM((BLOCK_ROWS, HEADS_W), BF16),
            pltpu.VMEM((2, BLOCK_ROWS, 128, HEAD_DIM), BF16),
            pltpu.VMEM((KVHEADS * HEADS_W, COLS), BF16),
            pltpu.VMEM((UP_SLOTS, 2, D, FF_STEP), BF16),
            pltpu.VMEM((DOWN_SLOTS, FF_LOCAL, PAIR), BF16),
            pltpu.VMEM((BLOCK_ROWS, 8, HEAD_DIM), F32),
            pltpu.VMEM((BLOCK_ROWS, 8, 128), jnp.int32),
            pltpu.VMEM((DEVS, BLOCK_ROWS, HEADS_W), BF16),
            pltpu.VMEM((EXPERTS * SLOTS, 128), F32),
            pltpu.VMEM((128, HALF_W), F32),
            pltpu.VMEM((EXPERTS, SLOTS, HALF_W), BF16),
            pltpu.VMEM((2, CHIPS, SLOTS, HALF_W), BF16),
            pltpu.VMEM((8, 128), F32),
            pltpu.VMEM((2, CHIPS, 8, 128), F32),
            pltpu.VMEM((SLOTS, D), BF16),
            pltpu.VMEM((SLOTS, FF_LOCAL), BF16),
            pltpu.VMEM((CHIPS, SLOTS, PAIR), BF16),
            pltpu.VMEM((2, CHIPS, SLOTS, HALF_W), BF16),
            dma((3,)),
            dma((UP_SLOTS, 2)),
            dma((DOWN_SLOTS,)),
            dma((DEVS,)),
            dma((DEVS,)),
            dma((DEVS,)),
            dma((DEVS,)),
            dma((DEVS,)),
            dma((DEVS,)),
            dma((CHIPS, 2)),
            dma((DEVS,)),
        ],
        compiler_params=pltpu.CompilerParams(
            collective_id=0, has_side_effects=True, vmem_limit_bytes=62 * 1024 * 1024
        ),
        cost_estimate=pl.CostEstimate(
            flops=2 * SLOTS * 3 * D * FF_LOCAL, bytes_accessed=6 * D * FF_LOCAL, transcendentals=0
        ),
    )(
        lengths,
        expert_ids,
        residual,
        norm_gain.reshape(1, COLS),
        router_weight,
        queries,
        kv_cache,
        out_weight,
        gate_weight,
        up_weight,
        down_weight,
    )


def solution(mesh):
    body = fused if mesh.shape["dev"] == DEVS else on_device
    in_specs = (
        P("groups", "dev"),
        P(("groups", "dev"), None, None),
        P(("groups", "dev"), None, None, None, None),
        P("groups"),
        P(None, "dev"),
        P("dev"),
        P("dev", None),
        P(None, "dev"),
        P(None, "dev"),
        P("dev", None),
        P("groups", None),
    )
    out_specs = P("groups", "dev")
    return jax.shard_map(
        body, mesh=mesh, in_specs=in_specs, out_specs=out_specs, check_vma=False
    )
```

```python
import math

import jax
import jax.numpy as jnp
from jax import lax
from jax.experimental import pallas as pl
from jax.experimental.pallas import tpu as pltpu
from jax.sharding import PartitionSpec as P

D = 3072
KVHEADS = 8
HEAD_DIM = 128
EXPERTS = 8
GROUP_Q = 6


def attend(query_block, cache_block, row_lengths):
    shard_rows = query_block.shape[0]
    query_heads = query_block.reshape(shard_rows, GROUP_Q, HEAD_DIM)
    key_block = cache_block[0]
    value_block = cache_block[1]
    scores = jnp.einsum(
        "thd,tld->thl", query_heads, key_block, preferred_element_type=jnp.float32
    ) / math.sqrt(HEAD_DIM)
    positions = jnp.arange(key_block.shape[1])
    valid = positions[None, None, :] < row_lengths[:, None, None]
    scores = jnp.where(valid, scores, -1e30)
    row_top = jnp.max(scores, axis=2, keepdims=True)
    expo = jnp.where(valid, jnp.exp(scores - row_top), 0.0)
    probs = (expo / jnp.sum(expo, axis=2, keepdims=True)).astype(jnp.bfloat16)
    mixed_heads = jnp.einsum("thl,tld->thd", probs, value_block, preferred_element_type=jnp.float32)
    return mixed_heads.reshape(shard_rows, GROUP_Q * HEAD_DIM).astype(jnp.bfloat16)


def slot_tables(expert_ids, logits, slot_count):
    numbers = jnp.arange(EXPERTS)
    pick_first = (expert_ids[:, 0:1] == numbers[None, :]).astype(jnp.float32)
    pick_second = (expert_ids[:, 1:2] == numbers[None, :]).astype(jnp.float32)
    logit_first = jnp.sum(logits * pick_first, axis=1)
    logit_second = jnp.sum(logits * pick_second, axis=1)
    gate_first = 1.0 / (1.0 + jnp.exp(logit_second - logit_first))
    gate_second = 1.0 / (1.0 + jnp.exp(logit_first - logit_second))
    routed = pick_first + pick_second
    gate_table = pick_first * gate_first[:, None] + pick_second * gate_second[:, None]
    ranks = jnp.cumsum(routed, axis=0) - routed
    slot_numbers = jnp.arange(slot_count).astype(jnp.float32)
    slot_table = routed.T[:, None, :] * (ranks.T[:, None, :] == slot_numbers[None, :, None]).astype(
        jnp.float32
    )
    slot_gate = jnp.einsum("esb,be->es", slot_table, gate_table, precision=lax.Precision.HIGHEST)
    return (slot_table, slot_gate)


def integer_ranks(expert_ids):
    numbers = jnp.arange(EXPERTS, dtype=jnp.int32)
    routed_int = (expert_ids[:, 0:1] == numbers[None, :]).astype(jnp.int32) + (
        expert_ids[:, 1:2] == numbers[None, :]
    ).astype(jnp.int32)
    ranks_int = jnp.cumsum(routed_int, axis=0) - routed_int
    return (routed_int, ranks_int)


def run_expert(slot_in, gate_weight, up_weight, down_weight, weights_here):
    gate_part = jnp.dot(slot_in, gate_weight, preferred_element_type=jnp.float32)
    up_part = jnp.dot(slot_in, up_weight, preferred_element_type=jnp.float32)
    activation = (jax.nn.silu(gate_part) * up_part).astype(jnp.bfloat16)
    expert_out = jnp.dot(activation, down_weight, preferred_element_type=jnp.float32)
    return expert_out * weights_here[:, None]


def on_device(
    residual,
    queries,
    kv_cache,
    lengths,
    out_weight,
    norm_gain,
    router_weight,
    gate_weight,
    up_weight,
    down_weight,
    expert_ids,
):
    devices = lax.axis_size("dev")
    my_index = lax.axis_index("dev")
    shard_rows = queries.shape[1]
    group_width = queries.shape[2]
    batch_rows = residual.shape[0]
    column_count = residual.shape[1]
    slot_count = batch_rows // 2
    per_expert = devices // EXPERTS
    my_expert = my_index // per_expert
    row_lengths = lax.dynamic_slice_in_dim(lengths, my_index // KVHEADS * shard_rows, shard_rows)
    heads_local = attend(queries[0], kv_cache[0], row_lengths)
    gathered = lax.all_gather(heads_local, "dev", axis=0, tiled=True)
    gathered = gathered.reshape(devices // KVHEADS, KVHEADS, shard_rows, group_width)
    weight_blocks = out_weight.reshape(KVHEADS, group_width, column_count)
    attended = jnp.einsum(
        "bgtk,gkc->btc", gathered, weight_blocks, preferred_element_type=jnp.float32
    )
    attended = attended.reshape(batch_rows, column_count)
    hidden_state = residual.astype(jnp.float32) + attended
    gain_cols = norm_gain.astype(jnp.float32)[None, :]
    router_cols = router_weight.astype(jnp.float32)
    squares_local = jnp.sum(hidden_state * hidden_state, axis=1)
    square_total = lax.psum(squares_local, "dev")
    scale = lax.rsqrt(square_total / D + 1e-05)
    normed = hidden_state * scale[:, None] * gain_cols
    logits = lax.psum(jnp.dot(normed, router_cols, precision=lax.Precision.HIGHEST), "dev")
    expert_in = normed.astype(jnp.bfloat16)
    slot_table, slot_gate = slot_tables(expert_ids, logits, slot_count)
    routed_int, ranks_int = integer_ranks(expert_ids)
    weights_here = lax.dynamic_index_in_dim(slot_gate, my_expert, 0, keepdims=False)
    picked = jnp.einsum(
        "esb,bc->sec",
        slot_table.astype(jnp.bfloat16),
        expert_in,
        preferred_element_type=jnp.float32,
    ).astype(jnp.bfloat16)
    outgoing = jnp.broadcast_to(
        picked[:, :, None, :], (slot_count, EXPERTS, per_expert, column_count)
    )
    outgoing = outgoing.reshape(slot_count, devices * column_count)
    slot_in = lax.all_to_all(outgoing, "dev", split_axis=1, concat_axis=1, tiled=True)
    expert_out = run_expert(slot_in, gate_weight, up_weight, down_weight, weights_here)
    returned = lax.all_to_all(expert_out, "dev", split_axis=1, concat_axis=1, tiled=True)
    summed = jnp.sum(returned.reshape(slot_count, EXPERTS, per_expert, column_count), axis=2)
    first_expert = expert_ids[:, 0]
    second_expert = expert_ids[:, 1]
    first_rank = jnp.take_along_axis(ranks_int, first_expert[:, None], axis=1)[:, 0]
    second_rank = jnp.take_along_axis(ranks_int, second_expert[:, None], axis=1)[:, 0]
    moe = summed[first_rank, first_expert] + summed[second_rank, second_expert]
    return (hidden_state + moe).astype(jnp.bfloat16)


ZS = 4
YS = 2
CHIPS = ZS * YS
DEVS = 2 * CHIPS
ROWS = 64
SLOTS = 32
BLOCK_ROWS = 32
COLS = 192
PAIR = 2 * COLS
HALF_W = 256
HEADS_W = GROUP_Q * HEAD_DIM
FF_LOCAL = 4096
FF_STEP = 512
FF_STEPS = FF_LOCAL // FF_STEP
UP_SLOTS = 5
DOWN_SLOTS = 8
F32 = jnp.float32
BF16 = jnp.bfloat16
NT = (((1,), (1,)), ((), ()))


def iota(shape, dim):
    return lax.broadcasted_iota(jnp.int32, shape, dim)


def fused_kernel(
    lengths,
    ids,
    residual,
    gain,
    router,
    q_hbm,
    kv_hbm,
    ow_hbm,
    gate_hbm,
    up_hbm,
    down_hbm,
    out,
    q_in,
    kv,
    ow,
    gu,
    dn,
    qs,
    lens,
    ids_pad,
    heads,
    gt,
    summed,
    wide,
    picks,
    xb,
    stat_out,
    stats,
    xfull,
    act,
    rs,
    ret,
    in_sem,
    gu_sem,
    dn_sem,
    h_send,
    h_recv,
    x_send,
    x_recv,
    s_send,
    s_recv,
    r_send,
    r_recv,
):
    me = lax.axis_index("dev")
    core = lax.rem(me, 2)
    chip = me // 2
    y = lax.rem(chip, YS)
    z = chip // YS
    sibling = chip * 2 + (1 - core)

    def dev_of(zz, yy, cc):
        return (zz * YS + yy) * 2 + cc

    def remote(source, target, send, recv, device):
        return pltpu.make_async_remote_copy(
            src_ref=source,
            dst_ref=target,
            send_sem=send,
            recv_sem=recv,
            device_id={"dev": device},
            device_id_type=pl.DeviceIdType.MESH,
        )

    q_copy = pltpu.make_async_copy(q_hbm.at[0], q_in, in_sem.at[0])
    kv_copy = pltpu.make_async_copy(kv_hbm.at[0], kv, in_sem.at[1])
    ow_copy = pltpu.make_async_copy(ow_hbm, ow, in_sem.at[2])
    q_copy.start()
    kv_copy.start()
    ow_copy.start()

    barrier = pltpu.get_barrier_semaphore()
    for k in range(1, DEVS):
        pl.semaphore_signal(
            barrier,
            inc=1,
            device_id={"dev": lax.rem(me + k, DEVS)},
            device_id_type=pl.DeviceIdType.MESH,
        )

    def gu_copy(j, which):
        slot = lax.rem(j, UP_SLOTS)
        start = pl.multiple_of(j * FF_STEP, FF_STEP)
        origin = up_hbm if which else gate_hbm
        return pltpu.make_async_copy(
            origin.at[:, pl.ds(start, FF_STEP)], gu.at[slot, which], gu_sem.at[slot, which]
        )

    def down_chip(d):
        return lax.rem(chip + d + 1, CHIPS)

    def dn_copy(d):
        slot = lax.rem(d, DOWN_SLOTS)
        start = pl.multiple_of(down_chip(d) * PAIR, 128)
        return pltpu.make_async_copy(
            down_hbm.at[:, pl.ds(start, PAIR)], dn.at[slot], dn_sem.at[slot]
        )

    my_rows = (me // KVHEADS) * BLOCK_ROWS
    for t in range(BLOCK_ROWS):
        lens[t] = jnp.full((8, 128), lengths[my_rows + t], jnp.int32)

    ids_pad[...] = jnp.full_like(ids_pad, -1)
    ids_pad[0:2, 0:ROWS] = ids[...]
    expert = iota((128, 128), 0)
    routed = jnp.where((ids_pad[0:1, :] == expert) | (ids_pad[1:2, :] == expert), 1.0, 0.0)
    before = jnp.where(expert < iota((128, 128), 1), 1.0, 0.0).astype(BF16)
    routed_bf = routed.astype(BF16)
    rank = jnp.dot(routed_bf, before, preferred_element_type=F32)
    code = (routed * (rank + 1.0)).astype(BF16)
    place = iota((EXPERTS * SLOTS, 128), 0)
    owner = iota((EXPERTS * SLOTS, 128), 1) * SLOTS
    spread = jnp.where((place >= owner) & (place < owner + SLOTS), 1.0, 0.0).astype(BF16)
    spread_code = jnp.dot(spread, code, preferred_element_type=F32)
    slot_number = (jnp.bitwise_and(place, SLOTS - 1) + 1).astype(F32)
    gt[...] = jnp.where(spread_code == slot_number, 1.0, 0.0)

    q_copy.wait()
    qs[...] = jnp.zeros_like(qs)
    for j in range(GROUP_Q):
        qs[:, j, :] = q_in[:, j * HEAD_DIM : (j + 1) * HEAD_DIM].astype(F32)
    kv_copy.wait()
    ow_copy.wait()
    for j in range(UP_SLOTS):
        gu_copy(j, 0).start()
        gu_copy(j, 1).start()
    for d in range(DOWN_SLOTS):
        dn_copy(d).start()

    scores = jnp.einsum(
        "thd,tld->thl", qs[...].astype(BF16), kv[0], preferred_element_type=F32
    ) * (1.0 / math.sqrt(HEAD_DIM))
    valid = iota((BLOCK_ROWS, 8, 128), 2) < lens[...]
    scores = jnp.where(valid, scores, -1e30)
    top = jnp.max(scores, axis=2, keepdims=True)
    expo = jnp.where(valid, jnp.exp(scores - top), 0.0)
    probs = (expo / jnp.sum(expo, axis=2, keepdims=True)).astype(BF16)
    qs[...] = jnp.einsum("thl,tld->thd", probs, kv[1], preferred_element_type=F32)
    for j in range(GROUP_Q):
        heads[me, :, j * HEAD_DIM : (j + 1) * HEAD_DIM] = qs[:, j, :].astype(BF16)

    pl.semaphore_wait(barrier, DEVS - 1)

    def head_copy(block, number, device):
        return remote(
            heads.at[block], heads.at[block], h_send.at[number], h_recv.at[block], device
        )

    sent = []

    def send_heads(block, device):
        copy = head_copy(block, len(sent), device)
        copy.start()
        sent.append(copy)

    def project(block):
        at = pl.multiple_of(lax.rem(block, KVHEADS) * HEADS_W, HEADS_W)
        rows_at = pl.ds(pl.multiple_of(block // KVHEADS * BLOCK_ROWS, BLOCK_ROWS), BLOCK_ROWS)
        summed[rows_at, :] += lax.dot_general(
            heads[block], ow[:, pl.ds(at, HEADS_W)], NT, preferred_element_type=F32
        )

    for k in (2, 1, 3):
        send_heads(me, dev_of(lax.rem(z + k, ZS), y, core))
    send_heads(me, dev_of(z, 1 - y, core))
    send_heads(me, sibling)
    summed[...] = residual[...].astype(F32)
    project(me)
    for k in (1, 3, 2):
        block = dev_of(lax.rem(z + k, ZS), y, core)
        head_copy(block, 0, sibling).wait_recv()
        send_heads(block, dev_of(z, 1 - y, core))
        send_heads(block, sibling)
        project(block)
    for k in (0, 1, 3, 2):
        block = dev_of(lax.rem(z + k, ZS), 1 - y, core)
        head_copy(block, 0, sibling).wait_recv()
        send_heads(block, sibling)
        project(block)
    for yy in (y, 1 - y):
        for k in (0, 1, 3, 2):
            block = dev_of(lax.rem(z + k, ZS), yy, 1 - core)
            head_copy(block, 0, sibling).wait_recv()
            project(block)

    hidden = summed[...]
    gained = hidden * gain[...].astype(F32).reshape(1, COLS)

    wide[...] = jnp.zeros_like(wide)
    wide[0:ROWS, 0:COLS] = gained
    shifted = pltpu.roll(wide[...], core * 64, 1)
    picked = jnp.dot(gt[...].astype(BF16), shifted.astype(BF16), preferred_element_type=F32)
    picks[...] = picked.astype(BF16).reshape(EXPERTS, SLOTS, HALF_W)

    none = jnp.zeros_like(hidden)
    stat_out[...] = lax.dot_general(
        router[...].astype(F32),
        jnp.concatenate([gained, none], axis=0),
        NT,
        precision=lax.Precision.HIGHEST,
        preferred_element_type=F32,
    ) + lax.dot_general(
        jnp.ones((8, COLS), F32),
        jnp.concatenate([none, hidden * hidden], axis=0),
        NT,
        precision=lax.Precision.HIGHEST,
        preferred_element_type=F32,
    )

    sent_x = []

    def row_copies(cc, source_chip, source, stat_source, number, device):
        at = cc * CHIPS + source_chip
        return (
            remote(source, xb.at[cc, source_chip], x_send.at[number], x_recv.at[at], device),
            remote(stat_source, stats.at[cc, source_chip], s_send.at[number], s_recv.at[at], device),
        )

    def send_rows(cc, source_chip, source, stat_source, device):
        copies = row_copies(cc, source_chip, source, stat_source, len(sent_x), device)
        for copy in copies:
            copy.start()
        sent_x.append(copies)

    def wait_rows(cc, source_chip):
        for copy in row_copies(
            cc, source_chip, xb.at[cc, source_chip], stats.at[cc, source_chip], 0, sibling
        ):
            copy.wait_recv()

    for k in (4, 3, 5, 2, 6, 1, 7):
        to = lax.rem(chip + k, CHIPS)
        send_rows(core, chip, picks.at[to], stat_out, to * 2 + core)
    send_rows(core, chip, picks.at[chip], stat_out, sibling)
    xb[core, chip] = picks[chip]
    stats[core, chip] = stat_out[...]
    for k in (1, 7, 2, 6, 3, 5, 4):
        source_chip = lax.rem(chip + k, CHIPS)
        wait_rows(core, source_chip)
        send_rows(
            core,
            source_chip,
            xb.at[core, source_chip],
            stats.at[core, source_chip],
            sibling,
        )
    for k in (0, 1, 7, 2, 6, 3, 5, 4):
        wait_rows(1 - core, lax.rem(chip + k, CHIPS))

    for s in range(CHIPS):
        at = s * PAIR
        xfull[:, at : at + 128] = xb[0, s, :, 0:128]
        xfull[:, at + 128 : at + 256] = xb[0, s, :, 128:256] + xb[1, s, :, 0:128]
        xfull[:, at + 256 : at + 384] = xb[1, s, :, 128:256]
    total = jnp.sum(stats[...].reshape(DEVS, 8, 128), axis=0)
    total = jnp.concatenate([total, jnp.zeros((120, 128), F32)], axis=0)
    mine = gt[pl.ds(pl.multiple_of(chip * SLOTS, SLOTS), SLOTS), :]
    slot_logits = lax.dot_general(
        mine, total, NT, precision=lax.Precision.HIGHEST, preferred_element_type=F32
    )
    slot_squares = lax.dot_general(
        pltpu.roll(mine, 64, 1),
        total,
        NT,
        precision=lax.Precision.HIGHEST,
        preferred_element_type=F32,
    )
    scale = lax.rsqrt(slot_squares[:, 0:1] / D + 1e-05)
    slot_experts = lax.dot_general(
        mine.astype(BF16), routed_bf, NT, preferred_element_type=F32
    )
    number = iota((SLOTS, 128), 1)
    own_logit = jnp.sum(jnp.where(number == chip, slot_logits, 0.0), axis=1, keepdims=True)
    other_logit = jnp.sum(
        jnp.where(number == chip, 0.0, slot_logits * slot_experts), axis=1, keepdims=True
    )
    weight = 1.0 / (1.0 + jnp.exp((other_logit - own_logit) * scale))

    def up_step(j):
        slot = lax.rem(j, UP_SLOTS)
        gu_copy(j, 0).wait()
        gu_copy(j, 1).wait()
        rows_in = xfull[...]
        gate_part = jnp.dot(rows_in, gu[slot, 0], preferred_element_type=F32) * scale
        up_part = jnp.dot(rows_in, gu[slot, 1], preferred_element_type=F32) * scale
        silu = gate_part / (1.0 + jnp.exp(-gate_part))
        act[:, pl.ds(pl.multiple_of(j * FF_STEP, FF_STEP), FF_STEP)] = (silu * up_part).astype(BF16)

    @pl.loop(0, FF_STEPS - UP_SLOTS)
    def _(j):
        up_step(j)
        gu_copy(j + UP_SLOTS, 0).start()
        gu_copy(j + UP_SLOTS, 1).start()

    @pl.loop(FF_STEPS - UP_SLOTS, FF_STEPS)
    def _(j):
        up_step(j)

    def return_copy(d, cc):
        return remote(
            rs.at[d, :, cc * 128 : cc * 128 + HALF_W],
            ret.at[core, chip],
            r_send.at[d, cc],
            r_recv.at[core * CHIPS + chip],
            down_chip(d) * 2 + cc,
        )

    def down_step(d):
        dn_copy(d).wait()
        part = jnp.dot(act[...], dn[lax.rem(d, DOWN_SLOTS)], preferred_element_type=F32)
        rs[d] = (part * weight).astype(BF16)

    @pl.loop(0, CHIPS - DOWN_SLOTS)
    def _(d):
        down_step(d)
        return_copy(d, 0).start()
        return_copy(d, 1).start()
        dn_copy(d + DOWN_SLOTS).start()

    @pl.loop(CHIPS - DOWN_SLOTS, CHIPS - 1)
    def _(d):
        down_step(d)
        return_copy(d, 0).start()
        return_copy(d, 1).start()

    last = CHIPS - 1
    down_step(last)

    def to_sibling(lanes):
        return remote(
            rs.at[last, :, lanes],
            ret.at[core, chip],
            r_send.at[last, 0],
            r_recv.at[core * CHIPS + chip],
            sibling,
        )

    @pl.when(core == 0)
    def _():
        to_sibling(slice(128, 384)).start()
        ret[core, chip] = rs[last, :, 0:256]

    @pl.when(core == 1)
    def _():
        to_sibling(slice(0, 256)).start()
        ret[core, chip] = rs[last, :, 128:384]

    def wait_return(cc, source_chip):
        remote(
            rs.at[0, :, 0:HALF_W],
            ret.at[cc, source_chip],
            r_send.at[0, 0],
            r_recv.at[cc * CHIPS + source_chip],
            sibling,
        ).wait_recv()

    for k in range(1, CHIPS):
        for cc in range(2):
            wait_return(cc, lax.rem(chip + k, CHIPS))
    wait_return(1 - core, chip)

    table = jnp.transpose(gt[...])[0:ROWS].astype(BF16)
    moe = jnp.zeros((ROWS, HALF_W), F32)
    for cc in range(2):
        moe += jnp.dot(
            table, ret[cc].reshape(EXPERTS * SLOTS, HALF_W), preferred_element_type=F32
        )
    moe = pltpu.roll(moe, core * (HALF_W - 64), 1)
    out[...] = (hidden + moe[:, 0:COLS]).astype(BF16)

    for copy in sent:
        copy.wait_send()
    for copies in sent_x:
        for copy in copies:
            copy.wait_send()

    @pl.loop(0, last)
    def _(d):
        return_copy(d, 0).wait_send()
        return_copy(d, 1).wait_send()

    to_sibling(slice(0, 256)).wait_send()


def fused(
    residual,
    queries,
    kv_cache,
    lengths,
    out_weight,
    norm_gain,
    router_weight,
    gate_weight,
    up_weight,
    down_weight,
    expert_ids,
):
    vmem = pl.BlockSpec(memory_space=pltpu.VMEM)
    anywhere = pl.BlockSpec(memory_space=pl.ANY)
    dma = pltpu.SemaphoreType.DMA
    return pl.pallas_call(
        fused_kernel,
        out_shape=jax.ShapeDtypeStruct((ROWS, COLS), BF16),
        in_specs=[pl.BlockSpec(memory_space=pltpu.SMEM)] + [vmem] * 4 + [anywhere] * 6,
        out_specs=vmem,
        scratch_shapes=[
            pltpu.VMEM((BLOCK_ROWS, HEADS_W), BF16),
            pltpu.VMEM((2, BLOCK_ROWS, 128, HEAD_DIM), BF16),
            pltpu.VMEM((COLS, KVHEADS * HEADS_W), BF16),
            pltpu.VMEM((UP_SLOTS, 2, D, FF_STEP), BF16),
            pltpu.VMEM((DOWN_SLOTS, FF_LOCAL, PAIR), BF16),
            pltpu.VMEM((BLOCK_ROWS, 8, HEAD_DIM), F32),
            pltpu.VMEM((BLOCK_ROWS, 8, 128), jnp.int32),
            pltpu.VMEM((8, 128), jnp.int32),
            pltpu.VMEM((DEVS, BLOCK_ROWS, HEADS_W), BF16),
            pltpu.VMEM((EXPERTS * SLOTS, 128), F32),
            pltpu.VMEM((ROWS, COLS), F32),
            pltpu.VMEM((128, HALF_W), F32),
            pltpu.VMEM((EXPERTS, SLOTS, HALF_W), BF16),
            pltpu.VMEM((2, CHIPS, SLOTS, HALF_W), BF16),
            pltpu.VMEM((8, 128), F32),
            pltpu.VMEM((2, CHIPS, 8, 128), F32),
            pltpu.VMEM((SLOTS, D), BF16),
            pltpu.VMEM((SLOTS, FF_LOCAL), BF16),
            pltpu.VMEM((CHIPS, SLOTS, PAIR), BF16),
            pltpu.VMEM((2, CHIPS, SLOTS, HALF_W), BF16),
            dma((3,)),
            dma((UP_SLOTS, 2)),
            dma((DOWN_SLOTS,)),
            dma((DEVS,)),
            dma((DEVS,)),
            dma((DEVS,)),
            dma((DEVS,)),
            dma((DEVS,)),
            dma((DEVS,)),
            dma((CHIPS, 2)),
            dma((DEVS,)),
        ],
        compiler_params=pltpu.CompilerParams(
            collective_id=0, has_side_effects=True, vmem_limit_bytes=63 * 1024 * 1024
        ),
        cost_estimate=pl.CostEstimate(
            flops=2 * SLOTS * 3 * D * FF_LOCAL, bytes_accessed=6 * D * FF_LOCAL, transcendentals=0
        ),
    )(
        lengths,
        expert_ids.T,
        residual,
        norm_gain,
        router_weight.T,
        queries,
        kv_cache,
        out_weight.T,
        gate_weight,
        up_weight,
        down_weight,
    )


def solution(mesh):
    body = fused if mesh.shape["dev"] == DEVS else on_device
    in_specs = (
        P("groups", "dev"),
        P(("groups", "dev"), None, None),
        P(("groups", "dev"), None, None, None, None),
        P("groups"),
        P(None, "dev"),
        P("dev"),
        P("dev", None),
        P(None, "dev"),
        P(None, "dev"),
        P("dev", None),
        P("groups", None),
    )
    out_specs = P("groups", "dev")
    return jax.shard_map(
        body, mesh=mesh, in_specs=in_specs, out_specs=out_specs, check_vma=False
    )
```

```python
import math

import jax
import jax.numpy as jnp
from jax import lax
from jax.experimental import pallas as pl
from jax.experimental.pallas import tpu as pltpu
from jax.sharding import PartitionSpec as P

D = 3072
KVHEADS = 8
HEAD_DIM = 128
EXPERTS = 8
GROUP_Q = 6


def attend(query_block, cache_block, row_lengths):
    shard_rows = query_block.shape[0]
    query_heads = query_block.reshape(shard_rows, GROUP_Q, HEAD_DIM)
    key_block = cache_block[0]
    value_block = cache_block[1]
    scores = jnp.einsum(
        "thd,tld->thl", query_heads, key_block, preferred_element_type=jnp.float32
    ) / math.sqrt(HEAD_DIM)
    positions = jnp.arange(key_block.shape[1])
    valid = positions[None, None, :] < row_lengths[:, None, None]
    scores = jnp.where(valid, scores, -1e30)
    row_top = jnp.max(scores, axis=2, keepdims=True)
    expo = jnp.where(valid, jnp.exp(scores - row_top), 0.0)
    probs = (expo / jnp.sum(expo, axis=2, keepdims=True)).astype(jnp.bfloat16)
    mixed_heads = jnp.einsum("thl,tld->thd", probs, value_block, preferred_element_type=jnp.float32)
    return mixed_heads.reshape(shard_rows, GROUP_Q * HEAD_DIM).astype(jnp.bfloat16)


def slot_tables(expert_ids, logits, slot_count):
    numbers = jnp.arange(EXPERTS)
    pick_first = (expert_ids[:, 0:1] == numbers[None, :]).astype(jnp.float32)
    pick_second = (expert_ids[:, 1:2] == numbers[None, :]).astype(jnp.float32)
    logit_first = jnp.sum(logits * pick_first, axis=1)
    logit_second = jnp.sum(logits * pick_second, axis=1)
    gate_first = 1.0 / (1.0 + jnp.exp(logit_second - logit_first))
    gate_second = 1.0 / (1.0 + jnp.exp(logit_first - logit_second))
    routed = pick_first + pick_second
    gate_table = pick_first * gate_first[:, None] + pick_second * gate_second[:, None]
    ranks = jnp.cumsum(routed, axis=0) - routed
    slot_numbers = jnp.arange(slot_count).astype(jnp.float32)
    slot_table = routed.T[:, None, :] * (ranks.T[:, None, :] == slot_numbers[None, :, None]).astype(
        jnp.float32
    )
    slot_gate = jnp.einsum("esb,be->es", slot_table, gate_table, precision=lax.Precision.HIGHEST)
    return (slot_table, slot_gate)


def integer_ranks(expert_ids):
    numbers = jnp.arange(EXPERTS, dtype=jnp.int32)
    routed_int = (expert_ids[:, 0:1] == numbers[None, :]).astype(jnp.int32) + (
        expert_ids[:, 1:2] == numbers[None, :]
    ).astype(jnp.int32)
    ranks_int = jnp.cumsum(routed_int, axis=0) - routed_int
    return (routed_int, ranks_int)


def run_expert(slot_in, gate_weight, up_weight, down_weight, weights_here):
    gate_part = jnp.dot(slot_in, gate_weight, preferred_element_type=jnp.float32)
    up_part = jnp.dot(slot_in, up_weight, preferred_element_type=jnp.float32)
    activation = (jax.nn.silu(gate_part) * up_part).astype(jnp.bfloat16)
    expert_out = jnp.dot(activation, down_weight, preferred_element_type=jnp.float32)
    return expert_out * weights_here[:, None]


def on_device(
    residual,
    queries,
    kv_cache,
    lengths,
    out_weight,
    norm_gain,
    router_weight,
    gate_weight,
    up_weight,
    down_weight,
    expert_ids,
):
    devices = lax.axis_size("dev")
    my_index = lax.axis_index("dev")
    shard_rows = queries.shape[1]
    group_width = queries.shape[2]
    batch_rows = residual.shape[0]
    column_count = residual.shape[1]
    slot_count = batch_rows // 2
    per_expert = devices // EXPERTS
    my_expert = my_index // per_expert
    row_lengths = lax.dynamic_slice_in_dim(lengths, my_index // KVHEADS * shard_rows, shard_rows)
    heads_local = attend(queries[0], kv_cache[0], row_lengths)
    gathered = lax.all_gather(heads_local, "dev", axis=0, tiled=True)
    gathered = gathered.reshape(devices // KVHEADS, KVHEADS, shard_rows, group_width)
    weight_blocks = out_weight.reshape(KVHEADS, group_width, column_count)
    attended = jnp.einsum(
        "bgtk,gkc->btc", gathered, weight_blocks, preferred_element_type=jnp.float32
    )
    attended = attended.reshape(batch_rows, column_count)
    hidden_state = residual.astype(jnp.float32) + attended
    gain_cols = norm_gain.astype(jnp.float32)[None, :]
    router_cols = router_weight.astype(jnp.float32)
    squares_local = jnp.sum(hidden_state * hidden_state, axis=1)
    square_total = lax.psum(squares_local, "dev")
    scale = lax.rsqrt(square_total / D + 1e-05)
    normed = hidden_state * scale[:, None] * gain_cols
    logits = lax.psum(jnp.dot(normed, router_cols, precision=lax.Precision.HIGHEST), "dev")
    expert_in = normed.astype(jnp.bfloat16)
    slot_table, slot_gate = slot_tables(expert_ids, logits, slot_count)
    routed_int, ranks_int = integer_ranks(expert_ids)
    weights_here = lax.dynamic_index_in_dim(slot_gate, my_expert, 0, keepdims=False)
    picked = jnp.einsum(
        "esb,bc->sec",
        slot_table.astype(jnp.bfloat16),
        expert_in,
        preferred_element_type=jnp.float32,
    ).astype(jnp.bfloat16)
    outgoing = jnp.broadcast_to(
        picked[:, :, None, :], (slot_count, EXPERTS, per_expert, column_count)
    )
    outgoing = outgoing.reshape(slot_count, devices * column_count)
    slot_in = lax.all_to_all(outgoing, "dev", split_axis=1, concat_axis=1, tiled=True)
    expert_out = run_expert(slot_in, gate_weight, up_weight, down_weight, weights_here)
    returned = lax.all_to_all(expert_out, "dev", split_axis=1, concat_axis=1, tiled=True)
    summed = jnp.sum(returned.reshape(slot_count, EXPERTS, per_expert, column_count), axis=2)
    first_expert = expert_ids[:, 0]
    second_expert = expert_ids[:, 1]
    first_rank = jnp.take_along_axis(ranks_int, first_expert[:, None], axis=1)[:, 0]
    second_rank = jnp.take_along_axis(ranks_int, second_expert[:, None], axis=1)[:, 0]
    moe = summed[first_rank, first_expert] + summed[second_rank, second_expert]
    return (hidden_state + moe).astype(jnp.bfloat16)


ZS = 4
YS = 2
CHIPS = ZS * YS
DEVS = 2 * CHIPS
ROWS = 64
SLOTS = 32
BLOCK_ROWS = 32
COLS = 192
PAIR = 2 * COLS
HALF_W = 256
HEADS_W = GROUP_Q * HEAD_DIM
FF_LOCAL = 4096
FF_STEP = 512
FF_STEPS = FF_LOCAL // FF_STEP
UP_SLOTS = 6
DOWN_SLOTS = 6
F32 = jnp.float32
BF16 = jnp.bfloat16
NT = (((1,), (1,)), ((), ()))


def iota(shape, dim):
    return lax.broadcasted_iota(jnp.int32, shape, dim)


def fused_kernel(
    lengths,
    ids,
    residual,
    gain,
    router,
    q_hbm,
    kv_hbm,
    ow_hbm,
    gate_hbm,
    up_hbm,
    down_hbm,
    out,
    q_in,
    kv,
    ow,
    gu,
    dn,
    qs,
    lens,
    ids_pad,
    heads,
    gt,
    summed,
    wide,
    picks,
    xb,
    stat_out,
    stats,
    xfull,
    act,
    rs,
    ret,
    in_sem,
    gu_sem,
    dn_sem,
    h_send,
    h_recv,
    x_send,
    x_recv,
    s_send,
    s_recv,
    r_send,
    r_recv,
):
    me = lax.axis_index("dev")
    core = lax.rem(me, 2)
    chip = me // 2
    y = lax.rem(chip, YS)
    z = chip // YS
    sibling = chip * 2 + (1 - core)

    def dev_of(zz, yy, cc):
        return (zz * YS + yy) * 2 + cc

    def remote(source, target, send, recv, device):
        return pltpu.make_async_remote_copy(
            src_ref=source,
            dst_ref=target,
            send_sem=send,
            recv_sem=recv,
            device_id={"dev": device},
            device_id_type=pl.DeviceIdType.MESH,
        )

    q_copy = pltpu.make_async_copy(q_hbm.at[0], q_in, in_sem.at[0])
    kv_copy = pltpu.make_async_copy(kv_hbm.at[0], kv, in_sem.at[1])
    ow_copy = pltpu.make_async_copy(ow_hbm, ow, in_sem.at[2])
    q_copy.start()
    kv_copy.start()
    ow_copy.start()

    barrier = pltpu.get_barrier_semaphore()
    for k in range(1, DEVS):
        pl.semaphore_signal(
            barrier,
            inc=1,
            device_id={"dev": lax.rem(me + k, DEVS)},
            device_id_type=pl.DeviceIdType.MESH,
        )

    def gu_copy(j, which):
        slot = lax.rem(j, UP_SLOTS)
        start = pl.multiple_of(j * FF_STEP, FF_STEP)
        origin = up_hbm if which else gate_hbm
        return pltpu.make_async_copy(
            origin.at[:, pl.ds(start, FF_STEP)], gu.at[slot, which], gu_sem.at[slot, which]
        )

    def down_chip(d):
        return lax.rem(chip + d + 1, CHIPS)

    def dn_copy(d):
        slot = lax.rem(d, DOWN_SLOTS)
        start = pl.multiple_of(down_chip(d) * PAIR, 128)
        return pltpu.make_async_copy(
            down_hbm.at[:, pl.ds(start, PAIR)], dn.at[slot], dn_sem.at[slot]
        )

    my_rows = (me // KVHEADS) * BLOCK_ROWS
    for t in range(BLOCK_ROWS):
        lens[t] = jnp.full((8, 128), lengths[my_rows + t], jnp.int32)

    ids_pad[...] = jnp.full_like(ids_pad, -1)
    ids_pad[0:2, 0:ROWS] = ids[...]
    expert = iota((128, 128), 0)
    routed = jnp.where((ids_pad[0:1, :] == expert) | (ids_pad[1:2, :] == expert), 1.0, 0.0)
    before = jnp.where(expert < iota((128, 128), 1), 1.0, 0.0).astype(BF16)
    routed_bf = routed.astype(BF16)
    rank = jnp.dot(routed_bf, before, preferred_element_type=F32)
    code = (routed * (rank + 1.0)).astype(BF16)
    place = iota((EXPERTS * SLOTS, 128), 0)
    owner = iota((EXPERTS * SLOTS, 128), 1) * SLOTS
    spread = jnp.where((place >= owner) & (place < owner + SLOTS), 1.0, 0.0).astype(BF16)
    spread_code = jnp.dot(spread, code, preferred_element_type=F32)
    slot_number = (jnp.bitwise_and(place, SLOTS - 1) + 1).astype(F32)
    gt[...] = jnp.where(spread_code == slot_number, 1.0, 0.0)

    q_copy.wait()
    qs[...] = jnp.zeros_like(qs)
    for j in range(GROUP_Q):
        qs[:, j, :] = q_in[:, j * HEAD_DIM : (j + 1) * HEAD_DIM].astype(F32)
    kv_copy.wait()
    ow_copy.wait()
    for j in range(UP_SLOTS):
        gu_copy(j, 0).start()
        gu_copy(j, 1).start()
    for d in range(DOWN_SLOTS):
        dn_copy(d).start()

    scores = jnp.einsum(
        "thd,tld->thl", qs[...].astype(BF16), kv[0], preferred_element_type=F32
    ) * (1.0 / math.sqrt(HEAD_DIM))
    valid = iota((BLOCK_ROWS, 8, 128), 2) < lens[...]
    scores = jnp.where(valid, scores, -1e30)
    top = jnp.max(scores, axis=2, keepdims=True)
    expo = jnp.where(valid, jnp.exp(scores - top), 0.0)
    probs = (expo / jnp.sum(expo, axis=2, keepdims=True)).astype(BF16)
    qs[...] = jnp.einsum("thl,tld->thd", probs, kv[1], preferred_element_type=F32)
    for j in range(GROUP_Q):
        heads[me, :, j * HEAD_DIM : (j + 1) * HEAD_DIM] = qs[:, j, :].astype(BF16)

    pl.semaphore_wait(barrier, DEVS - 1)

    def head_copy(block, number, device):
        return remote(
            heads.at[block], heads.at[block], h_send.at[number], h_recv.at[block], device
        )

    sent = []

    def send_heads(block, device):
        copy = head_copy(block, len(sent), device)
        copy.start()
        sent.append(copy)

    def project(block):
        at = pl.multiple_of(lax.rem(block, KVHEADS) * HEADS_W, HEADS_W)
        rows_at = pl.ds(pl.multiple_of(block // KVHEADS * BLOCK_ROWS, BLOCK_ROWS), BLOCK_ROWS)
        summed[rows_at, :] += lax.dot_general(
            heads[block], ow[:, pl.ds(at, HEADS_W)], NT, preferred_element_type=F32
        )

    for k in (2, 1, 3):
        send_heads(me, dev_of(lax.rem(z + k, ZS), y, core))
    send_heads(me, dev_of(z, 1 - y, core))
    send_heads(me, sibling)
    summed[...] = residual[...].astype(F32)
    project(me)
    for k in (1, 3, 2):
        block = dev_of(lax.rem(z + k, ZS), y, core)
        head_copy(block, 0, sibling).wait_recv()
        send_heads(block, dev_of(z, 1 - y, core))
        send_heads(block, sibling)
        project(block)
    for k in (0, 1, 3, 2):
        block = dev_of(lax.rem(z + k, ZS), 1 - y, core)
        head_copy(block, 0, sibling).wait_recv()
        send_heads(block, sibling)
        project(block)
    for yy in (y, 1 - y):
        for k in (0, 1, 3, 2):
            block = dev_of(lax.rem(z + k, ZS), yy, 1 - core)
            head_copy(block, 0, sibling).wait_recv()
            project(block)

    hidden = summed[...]
    gained = hidden * gain[...].astype(F32).reshape(1, COLS)

    wide[...] = jnp.zeros_like(wide)
    wide[0:ROWS, 0:COLS] = gained
    shifted = pltpu.roll(wide[...], core * 64, 1)
    picked = jnp.dot(gt[...].astype(BF16), shifted.astype(BF16), preferred_element_type=F32)
    picks[...] = picked.astype(BF16).reshape(EXPERTS, SLOTS, HALF_W)

    sent_x = []

    def row_copies(cc, source_chip, source, stat_source, number, device):
        at = cc * CHIPS + source_chip
        return (
            remote(source, xb.at[cc, source_chip], x_send.at[number], x_recv.at[at], device),
            remote(stat_source, stats.at[cc, source_chip], s_send.at[number], s_recv.at[at], device),
        )

    def send_rows(cc, source_chip, source, stat_source, device, first=False):
        copies = row_copies(cc, source_chip, source, stat_source, len(sent_x), device)
        copies[0].start()
        if not first:
            copies[1].start()
        sent_x.append(copies)

    def wait_rows(cc, source_chip):
        for copy in row_copies(
            cc, source_chip, xb.at[cc, source_chip], stats.at[cc, source_chip], 0, sibling
        ):
            copy.wait_recv()

    for k in (4, 3, 5, 2, 6, 1, 7):
        to = lax.rem(chip + k, CHIPS)
        send_rows(core, chip, picks.at[to], stat_out, to * 2 + core, first=True)
    send_rows(core, chip, picks.at[chip], stat_out, sibling, first=True)
    none = jnp.zeros_like(hidden)
    stat_out[...] = lax.dot_general(
        router[...].astype(F32),
        jnp.concatenate([gained, none], axis=0),
        NT,
        precision=lax.Precision.HIGHEST,
        preferred_element_type=F32,
    ) + lax.dot_general(
        jnp.ones((8, COLS), F32),
        jnp.concatenate([none, hidden * hidden], axis=0),
        NT,
        precision=lax.Precision.HIGHEST,
        preferred_element_type=F32,
    )
    for copies in sent_x:
        copies[1].start()
    xb[core, chip] = picks[chip]
    stats[core, chip] = stat_out[...]
    for k in (1, 7, 2, 6, 3, 5, 4):
        source_chip = lax.rem(chip + k, CHIPS)
        wait_rows(core, source_chip)
        send_rows(
            core,
            source_chip,
            xb.at[core, source_chip],
            stats.at[core, source_chip],
            sibling,
        )
    for k in (0, 1, 7, 2, 6, 3, 5, 4):
        wait_rows(1 - core, lax.rem(chip + k, CHIPS))

    for s in range(CHIPS):
        at = s * PAIR
        xfull[:, at : at + 128] = xb[0, s, :, 0:128]
        xfull[:, at + 128 : at + 256] = xb[0, s, :, 128:256] + xb[1, s, :, 0:128]
        xfull[:, at + 256 : at + 384] = xb[1, s, :, 128:256]
    total = jnp.sum(stats[...].reshape(DEVS, 8, 128), axis=0)
    total = jnp.concatenate([total, jnp.zeros((120, 128), F32)], axis=0)
    mine = gt[pl.ds(pl.multiple_of(chip * SLOTS, SLOTS), SLOTS), :]
    slot_logits = lax.dot_general(
        mine, total, NT, precision=lax.Precision.HIGHEST, preferred_element_type=F32
    )
    slot_squares = lax.dot_general(
        pltpu.roll(mine, 64, 1),
        total,
        NT,
        precision=lax.Precision.HIGHEST,
        preferred_element_type=F32,
    )
    scale = lax.rsqrt(slot_squares[:, 0:1] / D + 1e-05)
    slot_experts = lax.dot_general(
        mine.astype(BF16), routed_bf, NT, preferred_element_type=F32
    )
    number = iota((SLOTS, 128), 1)
    own_logit = jnp.sum(jnp.where(number == chip, slot_logits, 0.0), axis=1, keepdims=True)
    other_logit = jnp.sum(
        jnp.where(number == chip, 0.0, slot_logits * slot_experts), axis=1, keepdims=True
    )
    weight = 1.0 / (1.0 + jnp.exp((other_logit - own_logit) * scale))

    def up_step(j):
        slot = lax.rem(j, UP_SLOTS)
        gu_copy(j, 0).wait()
        gu_copy(j, 1).wait()
        rows_in = xfull[...]
        gate_part = jnp.dot(rows_in, gu[slot, 0], preferred_element_type=F32) * scale
        up_part = jnp.dot(rows_in, gu[slot, 1], preferred_element_type=F32) * scale
        silu = gate_part / (1.0 + jnp.exp(-gate_part))
        act[:, pl.ds(pl.multiple_of(j * FF_STEP, FF_STEP), FF_STEP)] = (silu * up_part).astype(BF16)

    @pl.loop(0, FF_STEPS - UP_SLOTS)
    def _(j):
        up_step(j)
        gu_copy(j + UP_SLOTS, 0).start()
        gu_copy(j + UP_SLOTS, 1).start()

    @pl.loop(FF_STEPS - UP_SLOTS, FF_STEPS)
    def _(j):
        up_step(j)

    def return_copy(d, cc):
        return remote(
            rs.at[d, :, cc * 128 : cc * 128 + HALF_W],
            ret.at[core, chip],
            r_send.at[d, cc],
            r_recv.at[core * CHIPS + chip],
            down_chip(d) * 2 + cc,
        )

    def down_step(d):
        dn_copy(d).wait()
        part = jnp.dot(act[...], dn[lax.rem(d, DOWN_SLOTS)], preferred_element_type=F32)
        rs[d] = (part * weight).astype(BF16)

    @pl.loop(0, CHIPS - DOWN_SLOTS)
    def _(d):
        down_step(d)
        return_copy(d, 0).start()
        return_copy(d, 1).start()
        dn_copy(d + DOWN_SLOTS).start()

    @pl.loop(CHIPS - DOWN_SLOTS, CHIPS - 1)
    def _(d):
        down_step(d)
        return_copy(d, 0).start()
        return_copy(d, 1).start()

    last = CHIPS - 1
    down_step(last)

    def to_sibling(lanes):
        return remote(
            rs.at[last, :, lanes],
            ret.at[core, chip],
            r_send.at[last, 0],
            r_recv.at[core * CHIPS + chip],
            sibling,
        )

    @pl.when(core == 0)
    def _():
        to_sibling(slice(128, 384)).start()
        ret[core, chip] = rs[last, :, 0:256]

    @pl.when(core == 1)
    def _():
        to_sibling(slice(0, 256)).start()
        ret[core, chip] = rs[last, :, 128:384]

    def wait_return(cc, source_chip):
        remote(
            rs.at[0, :, 0:HALF_W],
            ret.at[cc, source_chip],
            r_send.at[0, 0],
            r_recv.at[cc * CHIPS + source_chip],
            sibling,
        ).wait_recv()

    for k in range(1, CHIPS):
        for cc in range(2):
            wait_return(cc, lax.rem(chip + k, CHIPS))
    wait_return(1 - core, chip)

    table = jnp.transpose(gt[...])[0:ROWS].astype(BF16)
    moe = jnp.zeros((ROWS, HALF_W), F32)
    for cc in range(2):
        moe += jnp.dot(
            table, ret[cc].reshape(EXPERTS * SLOTS, HALF_W), preferred_element_type=F32
        )
    moe = pltpu.roll(moe, core * (HALF_W - 64), 1)
    out[...] = (hidden + moe[:, 0:COLS]).astype(BF16)

    for copy in sent:
        copy.wait_send()
    for copies in sent_x:
        for copy in copies:
            copy.wait_send()

    @pl.loop(0, last)
    def _(d):
        return_copy(d, 0).wait_send()
        return_copy(d, 1).wait_send()

    to_sibling(slice(0, 256)).wait_send()


def fused(
    residual,
    queries,
    kv_cache,
    lengths,
    out_weight,
    norm_gain,
    router_weight,
    gate_weight,
    up_weight,
    down_weight,
    expert_ids,
):
    vmem = pl.BlockSpec(memory_space=pltpu.VMEM)
    anywhere = pl.BlockSpec(memory_space=pl.ANY)
    dma = pltpu.SemaphoreType.DMA
    return pl.pallas_call(
        fused_kernel,
        out_shape=jax.ShapeDtypeStruct((ROWS, COLS), BF16),
        in_specs=[pl.BlockSpec(memory_space=pltpu.SMEM)] + [vmem] * 4 + [anywhere] * 6,
        out_specs=vmem,
        scratch_shapes=[
            pltpu.VMEM((BLOCK_ROWS, HEADS_W), BF16),
            pltpu.VMEM((2, BLOCK_ROWS, 128, HEAD_DIM), BF16),
            pltpu.VMEM((COLS, KVHEADS * HEADS_W), BF16),
            pltpu.VMEM((UP_SLOTS, 2, D, FF_STEP), BF16),
            pltpu.VMEM((DOWN_SLOTS, FF_LOCAL, PAIR), BF16),
            pltpu.VMEM((BLOCK_ROWS, 8, HEAD_DIM), F32),
            pltpu.VMEM((BLOCK_ROWS, 8, 128), jnp.int32),
            pltpu.VMEM((8, 128), jnp.int32),
            pltpu.VMEM((DEVS, BLOCK_ROWS, HEADS_W), BF16),
            pltpu.VMEM((EXPERTS * SLOTS, 128), F32),
            pltpu.VMEM((ROWS, COLS), F32),
            pltpu.VMEM((128, HALF_W), F32),
            pltpu.VMEM((EXPERTS, SLOTS, HALF_W), BF16),
            pltpu.VMEM((2, CHIPS, SLOTS, HALF_W), BF16),
            pltpu.VMEM((8, 128), F32),
            pltpu.VMEM((2, CHIPS, 8, 128), F32),
            pltpu.VMEM((SLOTS, D), BF16),
            pltpu.VMEM((SLOTS, FF_LOCAL), BF16),
            pltpu.VMEM((CHIPS, SLOTS, PAIR), BF16),
            pltpu.VMEM((2, CHIPS, SLOTS, HALF_W), BF16),
            dma((3,)),
            dma((UP_SLOTS, 2)),
            dma((DOWN_SLOTS,)),
            dma((DEVS,)),
            dma((DEVS,)),
            dma((DEVS,)),
            dma((DEVS,)),
            dma((DEVS,)),
            dma((DEVS,)),
            dma((CHIPS, 2)),
            dma((DEVS,)),
        ],
        compiler_params=pltpu.CompilerParams(
            collective_id=0, has_side_effects=True, vmem_limit_bytes=63 * 1024 * 1024
        ),
        cost_estimate=pl.CostEstimate(
            flops=2 * SLOTS * 3 * D * FF_LOCAL, bytes_accessed=6 * D * FF_LOCAL, transcendentals=0
        ),
    )(
        lengths,
        expert_ids.T,
        residual,
        norm_gain,
        router_weight.T,
        queries,
        kv_cache,
        out_weight.T,
        gate_weight,
        up_weight,
        down_weight,
    )


def solution(mesh):
    body = fused if mesh.shape["dev"] == DEVS else on_device
    in_specs = (
        P("groups", "dev"),
        P(("groups", "dev"), None, None),
        P(("groups", "dev"), None, None, None, None),
        P("groups"),
        P(None, "dev"),
        P("dev"),
        P("dev", None),
        P(None, "dev"),
        P(None, "dev"),
        P("dev", None),
        P("groups", None),
    )
    out_specs = P("groups", "dev")
    return jax.shard_map(
        body, mesh=mesh, in_specs=in_specs, out_specs=out_specs, check_vma=False
    )
```
